32 devices in a mesh: lang: 4 (over x, core), seq: 8 (over z, y).
Axes of the slice: x: 2, y: 2, z: 4, core: 2. Of those that a mesh axis runs over, the one named last changes fastest.
Arguments:
- prompt_rows: bfloat16 [4096, 2048], P(('lang', 'seq')), may hold values from -6 to 6
- expert_ids: int32 [4096, 2], P(('lang', 'seq')), may hold values from 0 to 3, all different within a row; in each aligned block of 128 rows (0 to 127, 128 to 255, ...) at most 96 rows name the same one
- expert_gates: float32 [4096, 2], P(('lang', 'seq')), may hold values from 0.25 to 1
- w_gate: bfloat16 [4, 2048, 704], P('lang', 'seq'), may hold values from -0.125 to 0.125
- w_up: bfloat16 [4, 2048, 704], P('lang', 'seq'), may hold values from -0.125 to 0.125
- w_down: bfloat16 [4, 704, 2048], P('lang', None, 'seq'), may hold values from -0.21875 to 0.21875
- w_kv: bfloat16 [2048, 2, 1024], P(None, None, 'seq'), may hold values from -0.125 to 0.125
- prompt_lengths: int32 [8], P('lang'), may hold values from 128 to 512, as said below
- latent_q: bfloat16 [8, 512, 1024], P('lang', 'seq'), may hold values from -5 to 5
- latent_k: bfloat16 [8, 512, 1024], P('lang', 'seq'), may hold values from -5 to 5
- latent_v: bfloat16 [8, 512, 1024], P('lang', 'seq'), may hold values from -6 to 6
- grad_out: bfloat16 [8, 512, 1024], P('lang', 'seq'), may hold values from -6 to 6
Outputs:
- attended: bfloat16 [8, 512, 1024], P('lang', 'seq')
- grad_latent: bfloat16 [3, 8, 512, 1024], P(None, 'lang', 'seq')
- grad_wkv: float32 [2048, 2, 1024], P(None, None, 'seq')
The draws below stay inside these ranges and needn't reach their ends.
Inputs may be any that keep to these rules, and one draw needn't show every extreme that they name: `expert_ids`: in each aligned block of 128 rows (the rows of one device) no expert is named by more than 96 rows. `prompt_lengths`: the first of each group of 2 pages uses its whole prompt.
All inputs are finite; a program needn't handle non-finite values.
Results may differ from the reference program's by a relative error of at most 0.03.
Values may be sent and summed in bfloat16 or wider, within the bound.
No kernel may reach another device: no remote copies, remote signals or barrier semaphores. Data moves between devices by JAX's collectives and lax.ppermute only.
A program may use at most 128 MiB of HBM per device.

```python
import math
import jax
import jax.numpy as jnp
import numpy as np
from jax import lax

D = 2048
FF = 704
HD = 128
TOP = 2
PAGES = 2
PROMPT_DEV = 128
EXPERTS = 4
CAP = 96
HEADS = 8
PROMPT = 512
LAT = 512
PAGE_ALL = 8
PTOK = 4096
N_LANG = 4


def draw_latent_q(key, part):
    key = jax.random.fold_in(key, 3)
    shape = (PAGES * N_LANG, LAT, HEADS * HD)
    base = jnp.clip(jax.random.normal(key, shape, jnp.float32), -5.0, 5.0)
    return base.astype(jnp.bfloat16)


def draw_latent_k(key, part):
    key = jax.random.fold_in(key, 5)
    shape = (PAGES * N_LANG, LAT, HEADS * HD)
    base = jnp.clip(jax.random.normal(key, shape, jnp.float32), -5.0, 5.0)
    return base.astype(jnp.bfloat16)


def draw_prompt_lengths(key, part):
    key = jax.random.fold_in(key, 7)
    page_count = PAGES * N_LANG
    lengths = jax.random.randint(key, (page_count,), PROMPT // 4, PROMPT + 1, dtype=jnp.int32)
    page_index = jnp.arange(page_count, dtype=jnp.int32)
    lengths = jnp.where(page_index % PAGES == 0, PROMPT, lengths)
    lengths = jnp.where(page_index == 1, PROMPT // 4, lengths)
    return lengths.astype(jnp.int32)


def steps_of(stream_key, dims, cuts, low, high):
    def one(axis_at, shards_of):
        draws = jax.random.uniform(jax.random.fold_in(jax.random.fold_in(stream_key, 6), axis_at), (shards_of,), jnp.float32, low / len(cuts), high / len(cuts))
        return jnp.repeat(jnp.exp(draws), dims[axis_at] // shards_of).reshape((-1,) + (1,) * (len(dims) - axis_at - 1))

    gain = one(*cuts[0])
    for cut in cuts[1:]:
        gain = gain * one(*cut)
    return gain


def shared_out(rng, own, number, rows, count, top, most, slope):
    order = jax.random.permutation(rng, count)
    crowded, usual = portions_of(count, rows * top, most, slope, True), portions_of(count, rows * top, most, slope, False)
    places = jnp.arange(count)

    def named(sizes, turn):
        used = int((sizes > 0).sum())
        fixed = max(1, used // 4)
        moved = fixed + (places - fixed + turn * (used - fixed)) % max(1, count - fixed)
        return jnp.zeros((count,), jnp.int32).at[order[jnp.where(places < fixed, places, moved)]].set(jnp.asarray(sizes, jnp.int32))

    sizes = jnp.where(number % 4 == 0, named(crowded, number // 4), named(usual, number - number // 4 - 1))
    mixed = jax.random.permutation(jax.random.fold_in(own, 3), count)
    source_of, receiver = mixed[0:count // 2 * 2:2], mixed[1:count // 2 * 2:2]
    room = jnp.minimum(sizes[source_of] - 1, most - sizes[receiver]) // 2
    room = jnp.where((source_of == order[0]) | (receiver == order[0]) | (sizes[receiver] == 0), 0, jnp.maximum(room, 0))
    moved = jax.random.randint(jax.random.fold_in(own, 4), (count // 2,), 0, 1 << 20) % (room + 1)
    sizes = sizes.at[source_of].add(-moved).at[receiver].add(moved)
    members = jnp.searchsorted(jnp.cumsum(sizes), jnp.arange(rows * top), side="right").astype(jnp.int32)
    listing = members.reshape(top, rows).T
    listing = listing[jax.random.permutation(jax.random.fold_in(own, 1), rows)]
    turn = jax.random.randint(jax.random.fold_in(own, 2), (rows, 1), 0, top)
    return jnp.take_along_axis(listing, (jnp.arange(top)[None, :] + turn) % top, axis=1)


def portions_of(number_of, total, limit, lean, full):
    loads = [(1 << 20) // math.isqrt(grade ** lean) + 1 for grade in range(1, number_of + 1)]
    largest = limit if full else min(limit, max(-(-total // number_of), total * loads[0] // sum(loads)))
    least = 1 if total - largest >= number_of - 1 else 0
    given, surplus = [largest] + [least] * (number_of - 1), total - largest - least * (number_of - 1)
    while surplus > 0:
        candidates = [i for i in range(1, number_of) if given[i] < largest] or [i for i in range(1, number_of) if given[i] < limit]
        mass, budget = sum([loads[i] for i in candidates]), surplus
        for i in candidates:
            addition = min(limit - given[i], max(1, budget * loads[i] // mass), surplus)
            given[i] = given[i] + addition
            surplus = surplus - addition
    return np.array(given)


def normal_values(own_key, extent, spread, reach, pieces=(), kind=jnp.bfloat16):
    drawn = jax.random.normal(own_key, extent, jnp.float32) * spread
    if len(pieces) > 0:
        drawn = steps_of(own_key, extent, pieces, -0.22, 0.18) * drawn
    return jnp.clip(drawn, min=-reach, max=reach).astype(kind)


def setup_inputs(seed: int = 0) -> dict:
    seeds = jax.random.split(jax.random.key(seed), 13)
    prompt_rows = normal_values(seeds[0], (PTOK, D), 1.0, 6.0, ((0, 32),))
    expert_ids_keys = jax.random.split(jax.random.fold_in(seeds[1], 1), PTOK // PROMPT_DEV)
    expert_ids_turns = jax.random.permutation(jax.random.fold_in(seeds[1], 3), PTOK // PROMPT_DEV)
    expert_ids = jax.vmap(lambda own, number: shared_out(jax.random.fold_in(seeds[1], 2), own, number, PROMPT_DEV, EXPERTS, TOP, CAP, 2))(expert_ids_keys, expert_ids_turns).reshape((PTOK, TOP))
    expert_gates = jnp.clip(jnp.exp(math.log(1.0) - 1.3862944 * jax.random.uniform(seeds[2], (PTOK, TOP), jnp.float32) ** steps_of(seeds[2], (PTOK, TOP), ((0, 32),), -0.2, 0.2)), 0.25, 1.0)
    w_gate = normal_values(seeds[3], (EXPERTS, D, FF), D ** -0.5, 0.125, ((0, 4), (1, 8)))
    w_up = normal_values(seeds[4], (EXPERTS, D, FF), D ** -0.5, 0.125, ((0, 4), (1, 8)))
    w_down = normal_values(seeds[5], (EXPERTS, FF, D), FF ** -0.5, 0.21875, ((0, 4), (2, 8)))
    w_kv = normal_values(seeds[6], (D, 2, HEADS * HD), D ** -0.5, 0.125, ((2, 8),))
    prompt_lengths = draw_prompt_lengths(jax.random.fold_in(seeds[12], 71), 0)
    latent_q = draw_latent_q(jax.random.fold_in(seeds[12], 71), 0)
    latent_k = draw_latent_k(jax.random.fold_in(seeds[12], 71), 0)
    latent_v = normal_values(seeds[10], (PAGE_ALL, LAT, HEADS * HD), 1.0, 6.0, ((0, 4), (1, 8)))
    grad_out = normal_values(seeds[11], (PAGE_ALL, LAT, HEADS * HD), 1.0, 6.0, ((0, 4), (1, 8)))
    return {"prompt_rows": prompt_rows, "expert_ids": expert_ids, "expert_gates": expert_gates, "w_gate": w_gate, "w_up": w_up, "w_down": w_down, "w_kv": w_kv, "prompt_lengths": prompt_lengths, "latent_q": latent_q, "latent_k": latent_k, "latent_v": latent_v, "grad_out": grad_out}


def expert_mixture(prompt_rows, expert_ids, expert_gates, w_gate, w_up, w_down):

    def one_expert(total, expert):
        gate_proj = jnp.dot(prompt_rows, w_gate[expert], preferred_element_type=jnp.float32)
        up_proj = jnp.dot(prompt_rows, w_up[expert], preferred_element_type=jnp.float32)
        hidden = (jax.nn.silu(gate_proj) * up_proj).astype(jnp.bfloat16)
        expert_out = jnp.dot(hidden, w_down[expert], preferred_element_type=jnp.float32).astype(jnp.bfloat16)
        weighting = lax.optimization_barrier(jnp.sum(jnp.where(expert_ids == expert, expert_gates, 0.0), axis=1))
        return (total + weighting[:, None] * expert_out.astype(jnp.float32), None)
    start_total = jnp.zeros(prompt_rows.shape, jnp.float32)
    total, unused = lax.scan(one_expert, start_total, jnp.arange(w_gate.shape[0], dtype=jnp.int32))
    return total.astype(jnp.bfloat16)

def joint_attention(queries, key_rows, values, key_valid, out_grads):
    rows_all, head_size = queries.shape
    block_rows = min(512, rows_all)
    blocks = rows_all // block_rows
    score_scale = 1.0 / math.sqrt(head_size)
    query_blocks = queries.reshape(blocks, block_rows, head_size)
    grad_blocks = out_grads.reshape(blocks, block_rows, head_size)

    def one_block(carry, inputs):
        key_grad, value_grad = carry
        query_block, grad_block = inputs
        scores = lax.dot_general(query_block, key_rows, (((1,), (1,)), ((), ())), preferred_element_type=jnp.float32) * score_scale
        scores = jnp.where(key_valid[None, :], scores, -jnp.inf)
        highest = lax.optimization_barrier(jnp.max(scores, axis=1, keepdims=True))
        raised = jnp.exp(scores - highest)
        soft_weights = raised / lax.optimization_barrier(jnp.sum(raised, axis=1, keepdims=True))
        soft_low = soft_weights.astype(jnp.bfloat16)
        attended = jnp.dot(soft_low, values, preferred_element_type=jnp.float32).astype(jnp.bfloat16)
        prob_grad = lax.dot_general(grad_block, values, (((1,), (1,)), ((), ())), preferred_element_type=jnp.float32)
        centre = lax.optimization_barrier(jnp.sum(soft_weights * prob_grad, axis=1, keepdims=True))
        score_grad = (soft_weights * (prob_grad - centre) * score_scale).astype(jnp.bfloat16)
        query_grad = jnp.dot(score_grad, key_rows, preferred_element_type=jnp.float32).astype(jnp.bfloat16)
        key_grad = key_grad + lax.dot_general(score_grad, query_block, (((0,), (0,)), ((), ())), preferred_element_type=jnp.float32)
        value_grad = value_grad + lax.dot_general(soft_low, grad_block, (((0,), (0,)), ((), ())), preferred_element_type=jnp.float32)
        return ((key_grad, value_grad), (attended, query_grad))
    empty_grad = jnp.zeros(key_rows.shape, jnp.float32)
    (key_grad, value_grad), (attended, query_grad) = lax.scan(one_block, (empty_grad, empty_grad), (query_blocks, grad_blocks))
    return (attended.reshape(rows_all, head_size), query_grad.reshape(rows_all, head_size), key_grad, value_grad)

def reference(prompt_rows, expert_ids, expert_gates, w_gate, w_up, w_down, w_kv, prompt_lengths, latent_q, latent_k, latent_v, grad_out):
    mixed = expert_mixture(prompt_rows, expert_ids, expert_gates, w_gate, w_up, w_down)
    page_total = PAGES * N_LANG
    kv_flat = jnp.dot(mixed, w_kv.reshape(D, 2 * HEADS * HD), preferred_element_type=jnp.float32).astype(jnp.bfloat16)
    prompt_kv = kv_flat.reshape(page_total, PROMPT, 2, HEADS, HD)
    positions = jnp.arange(PROMPT, dtype=jnp.int32)

    def heads_first(array):
        return array.reshape(page_total, LAT, HEADS, HD).transpose(0, 2, 1, 3)

    def one_page(inputs):
        query_page, key_page, value_page, grad_page, kv_page, length = inputs
        key_valid = jnp.concatenate([jnp.ones((LAT,), bool), positions < length])
        prompt_keys = kv_page[:, 0].transpose(1, 0, 2)
        prompt_values = kv_page[:, 1].transpose(1, 0, 2)

        def one_head(head_inputs):
            query_head, key_head, value_head, grad_head, prompt_key, prompt_value = head_inputs
            key_rows = jnp.concatenate([key_head, prompt_key], axis=0)
            value_rows = jnp.concatenate([value_head, prompt_value], axis=0)
            return joint_attention(query_head, key_rows, value_rows, key_valid, grad_head)
        return lax.map(one_head, (query_page, key_page, value_page, grad_page, prompt_keys, prompt_values))
    attended, query_grad, key_grad, value_grad = lax.map(one_page, (heads_first(latent_q), heads_first(latent_k), heads_first(latent_v), heads_first(grad_out), prompt_kv, prompt_lengths))

    def rows_first(array):
        return array.transpose(0, 2, 1, 3).reshape(page_total, LAT, HEADS * HD)
    latent_key = key_grad[:, :, :LAT].astype(jnp.bfloat16)
    latent_value = value_grad[:, :, :LAT].astype(jnp.bfloat16)
    grad_latent = jnp.stack([rows_first(query_grad), rows_first(latent_key), rows_first(latent_value)])
    prompt_key = key_grad[:, :, LAT:].astype(jnp.bfloat16).transpose(0, 2, 1, 3)
    prompt_value = value_grad[:, :, LAT:].astype(jnp.bfloat16).transpose(0, 2, 1, 3)
    prompt_grad = jnp.stack([prompt_key, prompt_value], axis=2).reshape(page_total * PROMPT, 2 * HEADS * HD)
    grad_wkv = lax.dot_general(mixed, prompt_grad, (((0,), (0,)), ((), ())), preferred_element_type=jnp.float32)
    return (rows_first(attended), grad_latent, grad_wkv.reshape(D, 2, HEADS * HD))
```

```python
import functools
import math

import jax
import jax.numpy as jnp
from jax import lax
from jax.experimental import pallas as pl
from jax.experimental.pallas import tpu as pltpu
from jax.sharding import PartitionSpec as P

HD = 128
PAIR = 2
TILE = 16
STEP = 4
NT = (((1,), (1,)), ((), ()))
TN = (((0,), (0,)), ((), ()))
F32 = jnp.float32
BF16 = jnp.bfloat16


def params():
    return pltpu.CompilerParams(vmem_limit_bytes=60 * 2**20)


def vmem():
    return pl.BlockSpec(memory_space=pltpu.VMEM)


def smem():
    return pl.BlockSpec(memory_space=pltpu.SMEM)


def dot(a, b):
    return jnp.dot(a, b, preferred_element_type=F32)


def ring_order(count):
    return list(range(0, count, 2)) + list(range(count - 1, 0, -2))


def ring_pairs(count, step):
    order = ring_order(count)
    return [(order[i], order[(i + step) % count]) for i in range(count)]


def ring_places(count):
    order = ring_order(count)
    return jnp.array([[order.index(i) for i in range(count)], order], jnp.int32)


def ring_gather(block, count):
    ahead = ring_pairs(count, 1)
    back = ring_pairs(count, -1)
    half_rows = block.shape[0] // 2
    parts = [(0, [block])]
    up, down = block, block
    for distance in range(1, count // 2):
        up = lax.ppermute(up, "seq", ahead)
        down = lax.ppermute(down, "seq", back)
        parts.append((-distance, [up]))
        parts.append((distance, [down]))
    last_up = lax.ppermute(up[:half_rows], "seq", ahead)
    last_down = lax.ppermute(down[half_rows:], "seq", back)
    parts.append((count // 2, [last_up, last_down]))
    return parts


def whole(refs):
    if len(refs) == 1:
        return refs[0][...]
    return jnp.concatenate([ref[...] for ref in refs], axis=0)


def xor_swap(array, axis, mask):
    count = lax.axis_size(axis)
    return lax.ppermute(array, axis, [(i, i ^ mask) for i in range(count)])


def gather_lang(rows, far):
    langs = lax.axis_size("lang")
    mask = langs // 2
    blocks = {0: rows, mask: far}
    while mask > 1:
        mask //= 2
        for lang, block in list(blocks.items()):
            blocks[lang | mask] = xor_swap(block, "lang", mask)
    return [blocks[lang] for lang in range(langs)]


def reduce_rows(keep, send, pair_first, after):
    langs = lax.axis_size("lang")

    def over_pair(parts):
        kept, sent = parts
        arrived = xor_swap(tie(sent.astype(BF16), after), "seq", PAIR)
        return kept + arrived.astype(F32)

    arrived = xor_swap(send, "lang", 1)
    halves = [keep[side].astype(F32) + arrived[side].astype(F32) for side in range(2)]
    if pair_first:
        halves = [over_pair(halves)]
    mask = 2
    while mask < langs:
        sent = jnp.stack([half[1::2] for half in halves]).astype(BF16)
        arrived = xor_swap(sent, "lang", mask).astype(F32)
        halves = [half[0::2] + arrived[side] for side, half in enumerate(halves)]
        mask *= 2
    total = halves[0] if pair_first else over_pair(halves)
    return total[0].astype(BF16)


def split_halves(block, seq_index):
    rows = block.shape[0] // 2
    side = (seq_index // PAIR) % 2
    mine = lax.dynamic_slice_in_dim(block, side * rows, rows, 0)
    other = lax.dynamic_slice_in_dim(block, (1 - side) * rows, rows, 0)
    return mine, other


def tie(array, *others):
    return lax.optimization_barrier((array, *others))[0]


def gather_inputs(gate, up, down, rows, seq_index, count, aside, own_sums):
    top = lax.axis_size("lang") // 2
    mine, other = zip(*[split_halves(block, seq_index) for block in (gate, up, down)])
    mine = jnp.concatenate(mine, axis=0)
    other = jnp.concatenate(other, axis=0)
    along, across = {0: mine}, {}
    along[2 * PAIR] = xor_swap(mine, "seq", 2 * PAIR)
    along[PAIR] = xor_swap(other, "seq", PAIR)
    across[1] = xor_swap(mine, "seq", 1)
    ready = [2 * PAIR, PAIR]
    pair_rows = far = rows
    for mask in range(3 * PAIR, count, PAIR):
        held = other if mask & PAIR else mine
        arrived = [along[done] for done in ready]
        held, pair_rows, far, across[1], aside, arrived = lax.optimization_barrier(
            (held, pair_rows, far, across[1], aside, arrived)
        )
        along[mask] = xor_swap(held, "seq", mask)
        for done, array in zip(ready, arrived):
            along[done] = array
            across[done | 1] = xor_swap(array, "seq", 1)
        if mask == 3 * PAIR:
            pair_rows = xor_swap(pair_rows, "seq", PAIR)
            far = xor_swap(far, "lang", top)
        ready = [mask]
    last = ready[0]
    early = [across[mask | 1] for mask in along if mask not in (0, last)]
    pair_rows, far, along[last], early = lax.optimization_barrier(
        (pair_rows, far, along[last], early)
    )
    for mask, array in zip([mask for mask in along if mask not in (0, last)], early):
        across[mask | 1] = array
    own_blocks = gather_lang(rows, far)
    first = sorted((along | across).items())
    first = [item for item in first if item[0] != last]
    sums = own_sums(own_blocks, first)
    across[last | 1], pair_far, sums = lax.optimization_barrier(
        (xor_swap(along[last], "seq", 1), xor_swap(pair_rows, "lang", top), sums)
    )
    pair_blocks = gather_lang(pair_rows, pair_far)
    late = [(mask, shard) for mask, shard in ((last, along[last]), (last | 1, across[last | 1]))]
    return along, across, own_blocks, pair_blocks, first, late, sums, aside


def pack_body(*refs):
    out = refs[-1]
    for which, ref in enumerate(refs[:-1]):
        for head in range(out.shape[0]):
            out[head, which] = ref[:, :, head * HD : (head + 1) * HD]


def pack(arrays):
    pages, rows, width = arrays[0].shape
    shape = (width // HD, len(arrays), pages, rows, HD)
    return pl.pallas_call(
        pack_body,
        out_shape=jax.ShapeDtypeStruct(shape, BF16),
        in_specs=[vmem()] * len(arrays),
        out_specs=vmem(),
        compiler_params=params(),
        name="pack",
    )(*arrays)


def unpack_body(packed, attended, grads):
    for head in range(packed.shape[0]):
        cols = slice(head * HD, (head + 1) * HD)
        attended[:, :, cols] = packed[head, 0]
        for which in range(3):
            grads[which, :, :, cols] = packed[head, which + 1]


def unpack(packed):
    heads, _, pages, rows, _ = packed.shape
    return pl.pallas_call(
        unpack_body,
        out_shape=(
            jax.ShapeDtypeStruct((pages, rows, heads * HD), BF16),
            jax.ShapeDtypeStruct((3, pages, rows, heads * HD), BF16),
        ),
        in_specs=[vmem()],
        out_specs=(vmem(), vmem()),
        compiler_params=params(),
        name="unpack",
    )(packed)


def with_gates(rows, expert_ids, expert_gates):
    picks = expert_ids.shape[1]
    fields = [expert_ids.T.astype(F32)]
    rest = expert_gates.T
    for _ in range(3):
        term = lax.reduce_precision(rest, 8, 7)
        fields.append(term)
        rest = rest - term
    tile = jnp.concatenate(fields, axis=0).astype(BF16)
    tile = jnp.pad(tile, ((0, TILE - 4 * picks), (0, rows.shape[1] - rows.shape[0])))
    return jnp.concatenate([rows, tile], axis=0)


def shard_sums(tokens, rows, seq, masks, shards):
    chunk = shards.shape[1] // len(masks)
    starts = [pl.multiple_of((seq ^ mask) * chunk, chunk) for mask in masks]
    inputs = [
        jnp.concatenate([ref[:rows, pl.ds(start, chunk)] for start in starts], axis=1)
        for ref in tokens
    ]
    inputs = jnp.concatenate(inputs, axis=0)
    return lax.dot_general(inputs, shards, NT, preferred_element_type=F32)


def beside(weights):
    both = 2 * (weights[0].shape[0] // 3)
    return jnp.concatenate([weight[:both, :] for weight in weights], axis=1)


def hidden_sums_stage(place, row_blocks, parts):
    blocks = len(row_blocks)
    rows = row_blocks[0].shape[0] - TILE
    masks = [mask for mask, _ in parts]

    def body(*refs):
        tokens, weights, out = refs[1 : 1 + blocks], refs[1 + blocks : -1], refs[-1]
        shards = beside(weights)
        for at in range(0, blocks, STEP):
            here = slice(at * rows, (at + STEP) * rows)
            out[here] = shard_sums(tokens[at : at + STEP], rows, refs[0][1], masks, shards)

    operands = [place, *row_blocks, *[array for _, array in parts]]
    shape = (rows * blocks, 2 * (parts[0][1].shape[0] // 3))
    return pl.pallas_call(
        body,
        out_shape=jax.ShapeDtypeStruct(shape, F32),
        in_specs=[smem()] + [vmem()] * (len(operands) - 1),
        out_specs=vmem(),
        compiler_params=params(),
        name="hidden_sums",
    )(*operands)


def expert_stage(place, own_blocks, pair_blocks, first, late, sums, picks):
    blocks = len(own_blocks)
    rows = own_blocks[0].shape[0] - TILE
    half = rows * blocks
    inner = sums.shape[1] // 2
    chunk = first[0][1].shape[1]
    parts = first + late
    width = chunk * len(parts) // 2

    def body(*refs):
        lang, seq = refs[0][0], refs[0][1]
        tokens = refs[1 : 1 + 2 * blocks]
        weights = refs[1 + 2 * blocks : -6]
        old, hidden = refs[-6], refs[-1]
        outs = refs[-5:-1]
        masks = [mask for mask, _ in parts]
        late_shards = beside(weights[len(first) :])
        shards = beside(weights)
        for at in range(0, 2 * blocks, STEP):
            group = tokens[at : at + STEP]
            if at < blocks:
                total = shard_sums(group, rows, seq, masks[len(first) :], late_shards)
                total = total + old[at * rows : (at + STEP) * rows]
            else:
                total = shard_sums(group, rows, seq, masks, shards)
            for block, ref in enumerate(group):
                fields = ref[rows:, :rows].astype(F32)
                weight = jnp.zeros((1, rows), F32)
                for pick in range(picks):
                    terms = [fields[row : row + 1] for row in range(pick, 4 * picks, picks)]
                    named = terms[0] == lang.astype(F32)
                    weight = weight + jnp.where(named, terms[1] + terms[2] + terms[3], 0.0)
                weight = jnp.broadcast_to(weight, (rows, rows)).T[:, :1]
                gate = total[block * rows : (block + 1) * rows, :inner]
                result = total[block * rows : (block + 1) * rows, inner:] * weight
                here = slice((at + block) * rows, (at + block + 1) * rows)
                hidden[here] = (gate / (1.0 + jnp.exp(-gate)) * result).astype(BF16)
        for mask, down in sorted(zip(masks, weights), key=lambda item: item[0]):
            slot = ((mask & ~1) ^ (seq & PAIR)) // 2
            cols = pl.ds(pl.multiple_of(slot * chunk, chunk), chunk)
            for at in range(0, 2 * blocks, 2 * STEP):
                here = hidden[at * rows : (at + 2 * STEP) * rows]
                result = dot(here, down[2 * inner :, :]).astype(BF16)
                for block in range(at, at + 2 * STEP):
                    target = outs[2 * (mask & 1) + block % 2]
                    piece = result[(block - at) * rows : (block - at + 1) * rows]
                    target[block // blocks, block % blocks // 2, :, cols] = piece

    arrays = [array for _, array in parts]
    operands = [place, *own_blocks, *pair_blocks, *arrays, sums]
    shape = jax.ShapeDtypeStruct((2, blocks // 2, rows, width), BF16)
    return pl.pallas_call(
        body,
        out_shape=(shape,) * 4,
        in_specs=[smem()] + [vmem()] * (len(operands) - 1),
        out_specs=(vmem(),) * 4,
        scratch_shapes=[pltpu.VMEM((2 * half, inner), BF16)],
        compiler_params=params(),
        name="expert",
    )(*operands)


def flatten(parts):
    return [array for _, arrays in parts for array in arrays]


def regroup(parts, refs):
    refs = list(refs)
    found = []
    for offset, arrays in parts:
        found.append((offset, refs[: len(arrays)]))
        refs = refs[len(arrays) :]
    return found


def attention_stage(place, table, lengths, latents, w_kv, groups):
    count, _, pages, rows, _ = latents.shape
    width = w_kv.shape[0]
    chunk = width // count
    block_rows = groups[0][1][0][1][0].shape[0]
    tokens = block_rows * count
    prompt = tokens // pages
    lat = rows * count
    keys_all = lat + prompt
    per_block = max(1, min(count, 256 * 1024 // (keys_all * rows)))
    query_rows = per_block * rows
    scale = 1.0 / math.sqrt(HD)
    rate = scale * math.log2(math.e)
    flat = [flatten(parts) for _, parts in groups]

    def body(*refs):
        own, places, used, packed, w_ref = refs[:5]
        rest = list(refs[5:])
        out, grads, mixed, prompt_grad, keys, values, key_grad, value_grad, acc = rest[-9:]
        own_place = places[0, own[1]]
        for (masks, parts), arrays in zip(groups, flat):
            for source, part_refs in regroup(parts, rest[: len(arrays)]):
                owner = places[1, (own_place + source + count) % count]
                place = pl.multiple_of(owner * block_rows, block_rows)
                for index, mask in enumerate(masks):
                    start = pl.multiple_of(((owner & ~PAIR) ^ mask) * chunk, chunk)
                    cols = slice(index * chunk, (index + 1) * chunk)
                    piece = jnp.concatenate([ref[:, cols] for ref in part_refs], axis=0)
                    mixed[pl.ds(place, block_rows), pl.ds(start, chunk)] = piece
            rest = rest[len(arrays) :]
        projected = dot(mixed[...], w_ref[...]).astype(BF16)
        for page in range(pages):
            at = slice(page * prompt, (page + 1) * prompt)
            keys[page, :lat] = packed[:, 1, page].reshape(lat, HD)
            values[page, :lat] = packed[:, 2, page].reshape(lat, HD)
            keys[page, lat:] = projected[at, :HD]
            values[page, lat:] = projected[at, HD:]

        def one_block(step, carry):
            block = pl.ds(step * per_block, per_block)
            for page in range(pages):
                query = packed[block, 0, page].reshape(query_rows, HD)
                grad = packed[block, 3, page].reshape(query_rows, HD)
                key = keys[page]
                value = values[page]
                scores = lax.dot_general(key, query, NT, preferred_element_type=F32)
                position = lax.broadcasted_iota(jnp.int32, (prompt, query_rows), 0)
                used_scores = jnp.where(position < used[page], scores[lat:], -jnp.inf)
                scores = jnp.concatenate([scores[:lat], used_scores], axis=0)
                highest = jnp.max(scores, axis=0, keepdims=True)
                raised = jnp.exp2((scores - highest) * rate)
                soft = raised * (1.0 / jnp.sum(raised, axis=0, keepdims=True))
                low = soft.astype(BF16)
                prob = lax.dot_general(value, grad, NT, preferred_element_type=F32)
                centre = jnp.sum(soft * prob, axis=0, keepdims=True)
                score_grad = (soft * (prob - centre) * scale).astype(BF16)
                attended = lax.dot_general(value, low, TN, preferred_element_type=F32).T
                query_grad = lax.dot_general(key, score_grad, TN, preferred_element_type=F32).T
                out[block, 0, page] = attended.astype(BF16).reshape(per_block, rows, HD)
                out[block, 1, page] = query_grad.astype(BF16).reshape(per_block, rows, HD)
                key_grad[page] += dot(score_grad, query)
                value_grad[page] += dot(low, grad)
            return carry

        key_grad[...] = jnp.zeros(key_grad.shape, F32)
        value_grad[...] = jnp.zeros(value_grad.shape, F32)
        lax.fori_loop(0, count // per_block, one_block, 0)
        for page in range(pages):
            out[:, 2, page] = key_grad[page, :lat].astype(BF16).reshape(count, rows, HD)
            out[:, 3, page] = value_grad[page, :lat].astype(BF16).reshape(count, rows, HD)
            at = slice(page * prompt, (page + 1) * prompt)
            prompt_grad[at, :HD] = key_grad[page, lat:].astype(BF16)
            prompt_grad[at, HD:] = value_grad[page, lat:].astype(BF16)
        total = lax.dot_general(mixed[...], prompt_grad[...], TN, preferred_element_type=F32)
        acc[pl.ds(0, width, stride=2), :] = total[:, :HD]
        acc[pl.ds(1, width, stride=2), :] = total[:, HD:]
        grads[...] = acc[...].astype(BF16)

    operands = [place, table, lengths, latents, w_kv]
    operands += [array for arrays in flat for array in arrays]
    return pl.pallas_call(
        body,
        out_shape=(
            jax.ShapeDtypeStruct(latents.shape, BF16),
            jax.ShapeDtypeStruct((2 * width, HD), BF16),
        ),
        in_specs=[smem()] * 3 + [vmem()] * (len(operands) - 3),
        out_specs=(vmem(),) * 2,
        scratch_shapes=[
            pltpu.VMEM((tokens, width), BF16),
            pltpu.VMEM((tokens, 2 * HD), BF16),
            pltpu.VMEM((pages, keys_all, HD), BF16),
            pltpu.VMEM((pages, keys_all, HD), BF16),
            pltpu.VMEM((pages, keys_all, HD), F32),
            pltpu.VMEM((pages, keys_all, HD), F32),
            pltpu.VMEM((2 * width, HD), F32),
        ],
        compiler_params=params(),
        name="attention",
    )(*operands)


def local(
    prompt_rows,
    expert_ids,
    expert_gates,
    w_gate,
    w_up,
    w_down,
    w_kv,
    prompt_lengths,
    latent_q,
    latent_k,
    latent_v,
    grad_out,
):
    count = lax.axis_size("seq")
    langs = lax.axis_size("lang")
    model_width = prompt_rows.shape[1]
    lang_index = lax.axis_index("lang")
    seq_index = lax.axis_index("seq")
    place = jnp.stack([lang_index, seq_index])
    picks = expert_ids.shape[1]

    packed = pack([latent_q, latent_k, latent_v, grad_out])
    kv_matrix = w_kv.reshape(model_width, 2 * HD)
    along, across, own_blocks, pair_blocks, first, late, sums, (packed, kv_matrix) = gather_inputs(
        w_gate[0].T,
        w_up[0].T,
        w_down[0],
        with_gates(prompt_rows, expert_ids, expert_gates),
        seq_index,
        count,
        (packed, kv_matrix),
        functools.partial(hidden_sums_stage, place),
    )
    packed = tie(packed, late[1][1])
    latents = lax.all_to_all(packed, "seq", split_axis=0, concat_axis=0, tiled=True)

    results = expert_stage(place, own_blocks, pair_blocks, first, late, sums, picks)
    groups = []
    for pair_first, members in enumerate((along, across)):
        keep, send = results[2 * pair_first : 2 * pair_first + 2]
        mixed = reduce_rows(keep, send, bool(pair_first), latents)
        groups.append((sorted(members), ring_gather(mixed, count)))

    out, part = attention_stage(
        place, ring_places(count), prompt_lengths, latents, kv_matrix, groups
    )
    returned = lax.all_to_all(out, "seq", split_axis=0, concat_axis=0, tiled=True)

    mask = langs // 2
    while mask > 1:
        part = (part.astype(F32) + xor_swap(part, "lang", mask).astype(F32)).astype(BF16)
        mask //= 2
    grad_wkv = part.astype(F32) + xor_swap(part, "lang", 1).astype(F32)
    grad_wkv = grad_wkv.reshape(model_width, 2, HD)
    attended, grad_latent = unpack(returned)
    return (attended, grad_latent, grad_wkv)


def solution(mesh):
    return jax.shard_map(
        local,
        mesh=mesh,
        in_specs=(
            P(("lang", "seq"), None),
            P(("lang", "seq"), None),
            P(("lang", "seq"), None),
            P("lang", "seq", None),
            P("lang", "seq", None),
            P("lang", None, "seq"),
            P(None, None, "seq"),
            P("lang"),
            P("lang", "seq", None),
            P("lang", "seq", None),
            P("lang", "seq", None),
            P("lang", "seq", None),
        ),
        out_specs=(P("lang", "seq", None), P(None, "lang", "seq", None), P(None, None, "seq")),
        check_vma=False,
    )
```

```python
import functools
import math

import jax
import jax.numpy as jnp
from jax import lax
from jax.experimental import pallas as pl
from jax.experimental.pallas import tpu as pltpu
from jax.sharding import PartitionSpec as P

HD = 128
PAIR = 2
TILE = 16
STEP = 4
NT = (((1,), (1,)), ((), ()))
TN = (((0,), (0,)), ((), ()))
F32 = jnp.float32
BF16 = jnp.bfloat16


def params():
    return pltpu.CompilerParams(vmem_limit_bytes=60 * 2**20)


def vmem():
    return pl.BlockSpec(memory_space=pltpu.VMEM)


def smem():
    return pl.BlockSpec(memory_space=pltpu.SMEM)


def dot(a, b):
    return jnp.dot(a, b, preferred_element_type=F32)


def ring_order(count):
    return list(range(0, count, 2)) + list(range(count - 1, 0, -2))


def ring_pairs(count, step):
    order = ring_order(count)
    return [(order[i], order[(i + step) % count]) for i in range(count)]


def ring_places(count):
    order = ring_order(count)
    return jnp.array([[order.index(i) for i in range(count)], order], jnp.int32)


def ring_gather(block, count):
    ahead = ring_pairs(count, 1)
    back = ring_pairs(count, -1)
    half_rows = block.shape[0] // 2
    parts = [(0, [block])]
    up, down = block, block
    for distance in range(1, count // 2):
        up = lax.ppermute(up, "seq", ahead)
        down = lax.ppermute(down, "seq", back)
        parts.append((-distance, [up]))
        parts.append((distance, [down]))
    last_up = lax.ppermute(up[:half_rows], "seq", ahead)
    last_down = lax.ppermute(down[half_rows:], "seq", back)
    parts.append((count // 2, [last_up, last_down]))
    return parts


def whole(refs):
    if len(refs) == 1:
        return refs[0][...]
    return jnp.concatenate([ref[...] for ref in refs], axis=0)


def xor_swap(array, axis, mask):
    count = lax.axis_size(axis)
    return lax.ppermute(array, axis, [(i, i ^ mask) for i in range(count)])


def gather_lang(rows, far):
    langs = lax.axis_size("lang")
    mask = langs // 2
    blocks = {0: rows, mask: far}
    while mask > 1:
        mask //= 2
        for lang, block in list(blocks.items()):
            blocks[lang | mask] = xor_swap(block, "lang", mask)
    return [blocks[lang] for lang in range(langs)]


def reduce_rows(keep, send, pair_first, after):
    langs = lax.axis_size("lang")

    def total(terms):
        return functools.reduce(lambda a, b: a + b, [term.astype(F32) for term in terms])

    def over_pair(terms):
        sent = tie(total([term[1:] for term in terms]).astype(BF16), after)
        return [term[:1] for term in terms] + [xor_swap(sent, "seq", PAIR)]

    terms = [keep, xor_swap(send, "lang", 1)]
    if pair_first:
        terms = over_pair(terms)
    mask = 2
    while mask < langs:
        sent = total([term[:, 1::2] for term in terms]).astype(BF16)
        terms = [term[:, 0::2] for term in terms] + [xor_swap(sent, "lang", mask)]
        mask *= 2
    if not pair_first:
        terms = over_pair(terms)
    return total(terms)[0, 0].astype(BF16)


def split_halves(block, seq_index):
    rows = block.shape[0] // 2
    side = (seq_index // PAIR) % 2
    mine = lax.dynamic_slice_in_dim(block, side * rows, rows, 0)
    other = lax.dynamic_slice_in_dim(block, (1 - side) * rows, rows, 0)
    return mine, other


def tie(array, *others):
    return lax.optimization_barrier((array, *others))[0]


def gather_inputs(gate, up, down, rows, seq_index, count, aside, own_sums):
    top = lax.axis_size("lang") // 2
    mine, other = zip(*[split_halves(block, seq_index) for block in (gate, up, down)])
    mine = jnp.concatenate(mine, axis=0)
    other = jnp.concatenate(other, axis=0)
    along, across = {0: mine}, {}
    along[2 * PAIR] = xor_swap(mine, "seq", 2 * PAIR)
    along[PAIR] = xor_swap(other, "seq", PAIR)
    across[1] = xor_swap(mine, "seq", 1)
    ready = [2 * PAIR, PAIR]
    pair_rows = far = rows
    for mask in range(3 * PAIR, count, PAIR):
        held = other if mask & PAIR else mine
        arrived = [along[done] for done in ready]
        held, pair_rows, far, across[1], aside, arrived = lax.optimization_barrier(
            (held, pair_rows, far, across[1], aside, arrived)
        )
        along[mask] = xor_swap(held, "seq", mask)
        for done, array in zip(ready, arrived):
            along[done] = array
            across[done | 1] = xor_swap(array, "seq", 1)
        if mask == 3 * PAIR:
            pair_rows = xor_swap(pair_rows, "seq", PAIR)
            far = xor_swap(far, "lang", top)
        ready = [mask]
    last = ready[0]
    early = [across[mask | 1] for mask in along if mask not in (0, last)]
    pair_rows, far, along[last], early = lax.optimization_barrier(
        (pair_rows, far, along[last], early)
    )
    for mask, array in zip([mask for mask in along if mask not in (0, last)], early):
        across[mask | 1] = array
    own_blocks = gather_lang(rows, far)
    first = sorted((along | across).items())
    first = [item for item in first if item[0] != last]
    sums = own_sums(own_blocks, first)
    across[last | 1], pair_far, sums = lax.optimization_barrier(
        (xor_swap(along[last], "seq", 1), xor_swap(pair_rows, "lang", top), sums)
    )
    pair_blocks = gather_lang(pair_rows, pair_far)
    late = [(mask, shard) for mask, shard in ((last, along[last]), (last | 1, across[last | 1]))]
    return along, across, own_blocks, pair_blocks, first, late, sums, aside


def pack_body(*refs):
    out = refs[-1]
    for which, ref in enumerate(refs[:-1]):
        for head in range(out.shape[0]):
            out[head, which] = ref[:, :, head * HD : (head + 1) * HD]


def pack(arrays):
    pages, rows, width = arrays[0].shape
    shape = (width // HD, len(arrays), pages, rows, HD)
    return pl.pallas_call(
        pack_body,
        out_shape=jax.ShapeDtypeStruct(shape, BF16),
        in_specs=[vmem()] * len(arrays),
        out_specs=vmem(),
        compiler_params=params(),
        name="pack",
    )(*arrays)


def unpack_body(packed, attended, grads):
    for head in range(packed.shape[0]):
        cols = slice(head * HD, (head + 1) * HD)
        attended[:, :, cols] = packed[head, 0]
        for which in range(3):
            grads[which, :, :, cols] = packed[head, which + 1]


def unpack(packed):
    heads, _, pages, rows, _ = packed.shape
    return pl.pallas_call(
        unpack_body,
        out_shape=(
            jax.ShapeDtypeStruct((pages, rows, heads * HD), BF16),
            jax.ShapeDtypeStruct((3, pages, rows, heads * HD), BF16),
        ),
        in_specs=[vmem()],
        out_specs=(vmem(), vmem()),
        compiler_params=params(),
        name="unpack",
    )(packed)


def with_gates(rows, expert_ids, expert_gates):
    picks = expert_ids.shape[1]
    fields = [expert_ids.T.astype(F32)]
    rest = expert_gates.T
    for _ in range(3):
        term = lax.reduce_precision(rest, 8, 7)
        fields.append(term)
        rest = rest - term
    tile = jnp.concatenate(fields, axis=0).astype(BF16)
    tile = jnp.pad(tile, ((0, TILE - 4 * picks), (0, rows.shape[1] - rows.shape[0])))
    return jnp.concatenate([rows, tile], axis=0)


def shard_sums(tokens, rows, seq, masks, shards):
    chunk = shards.shape[1] // len(masks)
    starts = [pl.multiple_of((seq ^ mask) * chunk, chunk) for mask in masks]
    inputs = [
        jnp.concatenate([ref[:rows, pl.ds(start, chunk)] for start in starts], axis=1)
        for ref in tokens
    ]
    inputs = jnp.concatenate(inputs, axis=0)
    return lax.dot_general(inputs, shards, NT, preferred_element_type=F32)


def beside(weights):
    both = 2 * (weights[0].shape[0] // 3)
    return jnp.concatenate([weight[:both, :] for weight in weights], axis=1)


def hidden_sums_stage(place, row_blocks, parts):
    blocks = len(row_blocks)
    rows = row_blocks[0].shape[0] - TILE
    masks = [mask for mask, _ in parts]

    def body(*refs):
        tokens, weights, out = refs[1 : 1 + blocks], refs[1 + blocks : -1], refs[-1]
        shards = beside(weights)
        for at in range(0, blocks, STEP):
            here = slice(at * rows, (at + STEP) * rows)
            out[here] = shard_sums(tokens[at : at + STEP], rows, refs[0][1], masks, shards)

    operands = [place, *row_blocks, *[array for _, array in parts]]
    shape = (rows * blocks, 2 * (parts[0][1].shape[0] // 3))
    return pl.pallas_call(
        body,
        out_shape=jax.ShapeDtypeStruct(shape, F32),
        in_specs=[smem()] + [vmem()] * (len(operands) - 1),
        out_specs=vmem(),
        compiler_params=params(),
        name="hidden_sums",
    )(*operands)


def expert_stage(place, own_blocks, pair_blocks, first, late, sums, picks):
    blocks = len(own_blocks)
    rows = own_blocks[0].shape[0] - TILE
    half = rows * blocks
    inner = sums.shape[1] // 2
    chunk = first[0][1].shape[1]
    parts = first + late
    width = chunk * len(parts) // 2

    def body(*refs):
        lang, seq = refs[0][0], refs[0][1]
        tokens = refs[1 : 1 + 2 * blocks]
        weights = refs[1 + 2 * blocks : -6]
        old, hidden = refs[-6], refs[-1]
        outs = refs[-5:-1]
        masks = [mask for mask, _ in parts]
        late_shards = beside(weights[len(first) :])
        shards = beside(weights)
        for at in range(0, 2 * blocks, STEP):
            group = tokens[at : at + STEP]
            if at < blocks:
                total = shard_sums(group, rows, seq, masks[len(first) :], late_shards)
                total = total + old[at * rows : (at + STEP) * rows]
            else:
                total = shard_sums(group, rows, seq, masks, shards)
            for block, ref in enumerate(group):
                fields = ref[rows:, :rows].astype(F32)
                weight = jnp.zeros((1, rows), F32)
                for pick in range(picks):
                    terms = [fields[row : row + 1] for row in range(pick, 4 * picks, picks)]
                    named = terms[0] == lang.astype(F32)
                    weight = weight + jnp.where(named, terms[1] + terms[2] + terms[3], 0.0)
                weight = jnp.broadcast_to(weight, (rows, rows)).T[:, :1]
                gate = total[block * rows : (block + 1) * rows, :inner]
                result = total[block * rows : (block + 1) * rows, inner:] * weight
                here = slice((at + block) * rows, (at + block + 1) * rows)
                hidden[here] = (gate / (1.0 + jnp.exp(-gate)) * result).astype(BF16)
        for mask, down in sorted(zip(masks, weights), key=lambda item: item[0]):
            slot = ((mask & ~1) ^ (seq & PAIR)) // 2
            cols = pl.ds(pl.multiple_of(slot * chunk, chunk), chunk)
            for at in range(0, 2 * blocks, 2 * STEP):
                here = hidden[at * rows : (at + 2 * STEP) * rows]
                result = dot(here, down[2 * inner :, :]).astype(BF16)
                for block in range(at, at + 2 * STEP):
                    target = outs[2 * (mask & 1) + block % 2]
                    piece = result[(block - at) * rows : (block - at + 1) * rows]
                    target[block // blocks, block % blocks // 2, :, cols] = piece

    arrays = [array for _, array in parts]
    operands = [place, *own_blocks, *pair_blocks, *arrays, sums]
    shape = jax.ShapeDtypeStruct((2, blocks // 2, rows, width), BF16)
    return pl.pallas_call(
        body,
        out_shape=(shape,) * 4,
        in_specs=[smem()] + [vmem()] * (len(operands) - 1),
        out_specs=(vmem(),) * 4,
        scratch_shapes=[pltpu.VMEM((2 * half, inner), BF16)],
        compiler_params=params(),
        name="expert",
    )(*operands)


def flatten(parts):
    return [array for _, arrays in parts for array in arrays]


def regroup(parts, refs):
    refs = list(refs)
    found = []
    for offset, arrays in parts:
        found.append((offset, refs[: len(arrays)]))
        refs = refs[len(arrays) :]
    return found


def attention_stage(place, table, lengths, latents, w_kv, groups, before=None):
    count, kinds, pages, rows, _ = latents.shape
    width = w_kv.shape[0]
    chunk = width // count
    near = count // pages
    block_rows = groups[0][1][0][1][0].shape[0]
    prompt = block_rows * near
    lat = rows * count
    keys_all = lat + prompt
    per_block = max(1, min(count, 256 * 1024 // (keys_all * rows)))
    query_rows = per_block * rows
    scale = 1.0 / math.sqrt(HD)
    rate = scale * math.log2(math.e)
    skipped = count // 2 if before is None else 0
    groups = [
        (masks, [part for part in parts if part[0] != skipped]) for masks, parts in groups
    ]
    flat = [flatten(parts) for _, parts in groups]
    old = [] if before is None else list(before)

    def body(*refs):
        own, places, used, packed, w_ref = refs[:5]
        old_refs = refs[5 : 5 + len(old)]
        rest = list(refs[5 + len(old) :])
        out, grads, mixed, prompt_grad, keys, values, key_grad, value_grad, acc = rest[-9:]
        own_place = places[0, own[1]]
        page = own[1] // near
        if old:
            page = pages - 1 - page
            out[:, :, own[1] // near] = old_refs[0][...]
        for (masks, parts), arrays in zip(groups, flat):
            for source, part_refs in regroup(parts, rest[: len(arrays)]):
                owner = places[1, (own_place + source + count) % count]
                at = pl.multiple_of(owner % near * block_rows, block_rows)

                @pl.when(owner // near == page)
                def _(masks=masks, part_refs=part_refs, owner=owner, at=at):
                    for index, mask in enumerate(masks):
                        start = pl.multiple_of(((owner & ~PAIR) ^ mask) * chunk, chunk)
                        cols = slice(index * chunk, (index + 1) * chunk)
                        piece = jnp.concatenate([ref[:, cols] for ref in part_refs], axis=0)
                        mixed[pl.ds(at, block_rows), pl.ds(start, chunk)] = piece

            rest = rest[len(arrays) :]
        projected = dot(mixed[...], w_ref[...]).astype(BF16)
        keys[:lat] = packed[:, 1, page].reshape(lat, HD)
        values[:lat] = packed[:, 2, page].reshape(lat, HD)
        keys[lat:] = projected[:, :HD]
        values[lat:] = projected[:, HD:]
        key_grad[...] = jnp.zeros(key_grad.shape, F32)
        value_grad[...] = jnp.zeros(value_grad.shape, F32)
        target = out.at[:, :, page] if old else out

        def one_block(step, carry):
            block = pl.ds(step * per_block, per_block)
            query = packed[block, 0, page].reshape(query_rows, HD)
            grad = packed[block, 3, page].reshape(query_rows, HD)
            key = keys[...]
            value = values[...]
            scores = lax.dot_general(key, query, NT, preferred_element_type=F32)
            position = lax.broadcasted_iota(jnp.int32, (prompt, query_rows), 0)
            used_scores = jnp.where(position < used[page], scores[lat:], -jnp.inf)
            scores = jnp.concatenate([scores[:lat], used_scores], axis=0)
            highest = jnp.max(scores, axis=0, keepdims=True)
            raised = jnp.exp2((scores - highest) * rate)
            soft = raised * (1.0 / jnp.sum(raised, axis=0, keepdims=True))
            low = soft.astype(BF16)
            prob = lax.dot_general(value, grad, NT, preferred_element_type=F32)
            centre = jnp.sum(soft * prob, axis=0, keepdims=True)
            score_grad = (soft * (prob - centre) * scale).astype(BF16)
            attended = lax.dot_general(value, low, TN, preferred_element_type=F32).T
            query_grad = lax.dot_general(key, score_grad, TN, preferred_element_type=F32).T
            target[block, 0] = attended.astype(BF16).reshape(per_block, rows, HD)
            target[block, 1] = query_grad.astype(BF16).reshape(per_block, rows, HD)
            key_grad[...] += dot(score_grad, query)
            value_grad[...] += dot(low, grad)
            return carry

        lax.fori_loop(0, count // per_block, one_block, 0, unroll=2)
        target[:, 2] = key_grad[:lat].astype(BF16).reshape(count, rows, HD)
        target[:, 3] = value_grad[:lat].astype(BF16).reshape(count, rows, HD)
        prompt_grad[:, :HD] = key_grad[lat:].astype(BF16)
        prompt_grad[:, HD:] = value_grad[lat:].astype(BF16)
        total = lax.dot_general(mixed[...], prompt_grad[...], TN, preferred_element_type=F32)
        if old:
            total = total + old_refs[1][...]
            acc[pl.ds(0, width, stride=2), :] = total[:, :HD]
            acc[pl.ds(1, width, stride=2), :] = total[:, HD:]
            grads[...] = acc[...].astype(BF16)
        else:
            grads[...] = total

    operands = [place, table, lengths, latents, w_kv, *old]
    operands += [array for arrays in flat for array in arrays]
    if old:
        out_shape = (
            jax.ShapeDtypeStruct(latents.shape, BF16),
            jax.ShapeDtypeStruct((2 * width, HD), BF16),
        )
    else:
        out_shape = (
            jax.ShapeDtypeStruct((count, kinds, rows, HD), BF16),
            jax.ShapeDtypeStruct((width, 2 * HD), F32),
        )
    return pl.pallas_call(
        body,
        out_shape=out_shape,
        in_specs=[smem()] * 3 + [vmem()] * (len(operands) - 3),
        out_specs=(vmem(),) * 2,
        scratch_shapes=[
            pltpu.VMEM((prompt, width), BF16),
            pltpu.VMEM((prompt, 2 * HD), BF16),
            pltpu.VMEM((keys_all, HD), BF16),
            pltpu.VMEM((keys_all, HD), BF16),
            pltpu.VMEM((keys_all, HD), F32),
            pltpu.VMEM((keys_all, HD), F32),
            pltpu.VMEM((2 * width, HD), F32),
        ],
        compiler_params=params(),
        name="attention",
    )(*operands)


def local(
    prompt_rows,
    expert_ids,
    expert_gates,
    w_gate,
    w_up,
    w_down,
    w_kv,
    prompt_lengths,
    latent_q,
    latent_k,
    latent_v,
    grad_out,
):
    count = lax.axis_size("seq")
    langs = lax.axis_size("lang")
    model_width = prompt_rows.shape[1]
    lang_index = lax.axis_index("lang")
    seq_index = lax.axis_index("seq")
    place = jnp.stack([lang_index, seq_index])
    picks = expert_ids.shape[1]

    packed = pack([latent_q, latent_k, latent_v, grad_out])
    kv_matrix = w_kv.reshape(model_width, 2 * HD)
    along, across, own_blocks, pair_blocks, first, late, sums, (packed, kv_matrix) = gather_inputs(
        w_gate[0].T,
        w_up[0].T,
        w_down[0],
        with_gates(prompt_rows, expert_ids, expert_gates),
        seq_index,
        count,
        (packed, kv_matrix),
        functools.partial(hidden_sums_stage, place),
    )
    packed = tie(packed, late[1][1])
    latents = lax.all_to_all(packed, "seq", split_axis=0, concat_axis=0, tiled=True)

    results = expert_stage(place, own_blocks, pair_blocks, first, late, sums, picks)
    groups = []
    for pair_first, members in enumerate((along, across)):
        keep, send = results[2 * pair_first : 2 * pair_first + 2]
        mixed = reduce_rows(keep, send, bool(pair_first), latents)
        groups.append((sorted(members), ring_gather(mixed, count)))

    table = ring_places(count)
    own_page = attention_stage(place, table, prompt_lengths, latents, kv_matrix, groups)
    out, part = attention_stage(
        place, table, prompt_lengths, latents, kv_matrix, groups, own_page
    )
    returned = lax.all_to_all(out, "seq", split_axis=0, concat_axis=0, tiled=True)

    mask = langs // 2
    while mask > 1:
        part = (part.astype(F32) + xor_swap(part, "lang", mask).astype(F32)).astype(BF16)
        mask //= 2
    grad_wkv = part.astype(F32) + xor_swap(part, "lang", 1).astype(F32)
    grad_wkv = grad_wkv.reshape(model_width, 2, HD)
    attended, grad_latent = unpack(returned)
    return (attended, grad_latent, grad_wkv)


def solution(mesh):
    return jax.shard_map(
        local,
        mesh=mesh,
        in_specs=(
            P(("lang", "seq"), None),
            P(("lang", "seq"), None),
            P(("lang", "seq"), None),
            P("lang", "seq", None),
            P("lang", "seq", None),
            P("lang", None, "seq"),
            P(None, None, "seq"),
            P("lang"),
            P("lang", "seq", None),
            P("lang", "seq", None),
            P("lang", "seq", None),
            P("lang", "seq", None),
        ),
        out_specs=(P("lang", "seq", None), P(None, "lang", "seq", None), P(None, None, "seq")),
        check_vma=False,
    )
```

```python
import functools
import math

import jax
import jax.numpy as jnp
from jax import lax
from jax.experimental import pallas as pl
from jax.experimental.pallas import tpu as pltpu
from jax.sharding import PartitionSpec as P

HD = 128
PAIR = 2
TILE = 16
STEP = 4
NT = (((1,), (1,)), ((), ()))
TN = (((0,), (0,)), ((), ()))
F32 = jnp.float32
BF16 = jnp.bfloat16


def params():
    return pltpu.CompilerParams(vmem_limit_bytes=60 * 2**20)


def vmem():
    return pl.BlockSpec(memory_space=pltpu.VMEM)


def smem():
    return pl.BlockSpec(memory_space=pltpu.SMEM)


def dot(a, b):
    return jnp.dot(a, b, preferred_element_type=F32)


def ring_order(count):
    return list(range(0, count, 2)) + list(range(count - 1, 0, -2))


def ring_pairs(count, step):
    order = ring_order(count)
    return [(order[i], order[(i + step) % count]) for i in range(count)]


def ring_places(count):
    order = ring_order(count)
    return jnp.array([[order.index(i) for i in range(count)], order], jnp.int32)


def ring_gather(block, count):
    ahead = ring_pairs(count, 1)
    back = ring_pairs(count, -1)
    half_rows = block.shape[0] // 2
    parts = [(0, [block])]
    up, down = block, block
    for distance in range(1, count // 2):
        up = lax.ppermute(up, "seq", ahead)
        down = lax.ppermute(down, "seq", back)
        parts.append((-distance, [up]))
        parts.append((distance, [down]))
    last_up = lax.ppermute(up[:half_rows], "seq", ahead)
    last_down = lax.ppermute(down[half_rows:], "seq", back)
    parts.append((count // 2, [last_up, last_down]))
    return parts


def whole(refs):
    if len(refs) == 1:
        return refs[0][...]
    return jnp.concatenate([ref[...] for ref in refs], axis=0)


def xor_swap(array, axis, mask):
    count = lax.axis_size(axis)
    return lax.ppermute(array, axis, [(i, i ^ mask) for i in range(count)])


def gather_lang(rows, far):
    langs = lax.axis_size("lang")
    mask = langs // 2
    blocks = {0: rows, mask: far}
    while mask > 1:
        mask //= 2
        for lang, block in list(blocks.items()):
            blocks[lang | mask] = xor_swap(block, "lang", mask)
    return [blocks[lang] for lang in range(langs)]


def reduce_rows(keep, send, pair_first, after):
    langs = lax.axis_size("lang")

    def total(terms):
        return functools.reduce(lambda a, b: a + b, [term.astype(F32) for term in terms])

    def over_pair(terms):
        sent = total([term[1:] for term in terms]).astype(BF16)
        return [term[:1] for term in terms] + [xor_swap(sent, "seq", PAIR)]

    terms = [keep, xor_swap(send, "lang", 1)]
    if pair_first:
        terms = over_pair(terms)
    mask = 2
    while mask < langs:
        sent = total([term[:, 1::2] for term in terms]).astype(BF16)
        if not pair_first and mask == 2:
            sent = tie(sent, after)
        terms = [term[:, 0::2] for term in terms] + [xor_swap(sent, "lang", mask)]
        mask *= 2
    if not pair_first:
        terms = over_pair(terms)
    return total(terms)[0, 0].astype(BF16)


def split_halves(block, seq_index):
    rows = block.shape[0] // 2
    side = (seq_index // PAIR) % 2
    mine = lax.dynamic_slice_in_dim(block, side * rows, rows, 0)
    other = lax.dynamic_slice_in_dim(block, (1 - side) * rows, rows, 0)
    return mine, other


def tie(array, *others):
    return lax.optimization_barrier((array, *others))[0]


def gather_inputs(gate, up, down, rows, seq_index, count, aside, own_sums):
    top = lax.axis_size("lang") // 2
    mine, other = zip(*[split_halves(block, seq_index) for block in (gate, up, down)])
    mine = jnp.concatenate(mine, axis=0)
    other = jnp.concatenate(other, axis=0)
    along, across = {0: mine}, {}
    along[2 * PAIR] = xor_swap(mine, "seq", 2 * PAIR)
    along[PAIR] = xor_swap(other, "seq", PAIR)
    across[1] = xor_swap(mine, "seq", 1)
    ready = [2 * PAIR, PAIR]
    pair_rows = far = rows
    for mask in range(3 * PAIR, count, PAIR):
        held = other if mask & PAIR else mine
        arrived = [along[done] for done in ready]
        held, pair_rows, far, across[1], aside, arrived = lax.optimization_barrier(
            (held, pair_rows, far, across[1], aside, arrived)
        )
        along[mask] = xor_swap(held, "seq", mask)
        for done, array in zip(ready, arrived):
            along[done] = array
            across[done | 1] = xor_swap(array, "seq", 1)
        if mask == 3 * PAIR:
            pair_rows = xor_swap(pair_rows, "seq", PAIR)
            far = xor_swap(far, "lang", top)
        ready = [mask]
    last = ready[0]
    early = [across[mask | 1] for mask in along if mask not in (0, last)]
    pair_rows, far, along[last], early = lax.optimization_barrier(
        (pair_rows, far, along[last], early)
    )
    for mask, array in zip([mask for mask in along if mask not in (0, last)], early):
        across[mask | 1] = array
    own_blocks = gather_lang(rows, far)
    first = sorted((along | across).items())
    first = [item for item in first if item[0] != last]
    sums = own_sums(own_blocks, first)
    across[last | 1], pair_far, sums = lax.optimization_barrier(
        (xor_swap(along[last], "seq", 1), xor_swap(pair_rows, "lang", top), sums)
    )
    pair_blocks = gather_lang(pair_rows, pair_far)
    late = [(mask, shard) for mask, shard in ((last, along[last]), (last | 1, across[last | 1]))]
    return along, across, own_blocks, pair_blocks, first, late, sums, aside


def pack_body(*refs):
    out = refs[-1]
    for which, ref in enumerate(refs[:-1]):
        for head in range(out.shape[0]):
            out[head, which] = ref[:, :, head * HD : (head + 1) * HD]


def pack(arrays):
    pages, rows, width = arrays[0].shape
    shape = (width // HD, len(arrays), pages, rows, HD)
    return pl.pallas_call(
        pack_body,
        out_shape=jax.ShapeDtypeStruct(shape, BF16),
        in_specs=[vmem()] * len(arrays),
        out_specs=vmem(),
        compiler_params=params(),
        name="pack",
    )(*arrays)


def unpack_body(packed, attended, grads):
    for head in range(packed.shape[0]):
        cols = slice(head * HD, (head + 1) * HD)
        attended[:, :, cols] = packed[head, 0]
        for which in range(3):
            grads[which, :, :, cols] = packed[head, which + 1]


def unpack(packed):
    heads, _, pages, rows, _ = packed.shape
    return pl.pallas_call(
        unpack_body,
        out_shape=(
            jax.ShapeDtypeStruct((pages, rows, heads * HD), BF16),
            jax.ShapeDtypeStruct((3, pages, rows, heads * HD), BF16),
        ),
        in_specs=[vmem()],
        out_specs=(vmem(), vmem()),
        compiler_params=params(),
        name="unpack",
    )(packed)


def with_gates(rows, expert_ids, expert_gates):
    picks = expert_ids.shape[1]
    fields = [expert_ids.T.astype(F32)]
    rest = expert_gates.T
    for _ in range(3):
        term = lax.reduce_precision(rest, 8, 7)
        fields.append(term)
        rest = rest - term
    tile = jnp.concatenate(fields, axis=0).astype(BF16)
    tile = jnp.pad(tile, ((0, TILE - 4 * picks), (0, rows.shape[1] - rows.shape[0])))
    return jnp.concatenate([rows, tile], axis=0)


def shard_sums(tokens, rows, seq, masks, shards):
    chunk = shards.shape[1] // len(masks)
    starts = [pl.multiple_of((seq ^ mask) * chunk, chunk) for mask in masks]
    inputs = [
        jnp.concatenate([ref[:rows, pl.ds(start, chunk)] for start in starts], axis=1)
        for ref in tokens
    ]
    inputs = jnp.concatenate(inputs, axis=0)
    return lax.dot_general(inputs, shards, NT, preferred_element_type=F32)


def beside(weights):
    both = 2 * (weights[0].shape[0] // 3)
    return jnp.concatenate([weight[:both, :] for weight in weights], axis=1)


def hidden_sums_stage(place, row_blocks, parts):
    blocks = len(row_blocks)
    rows = row_blocks[0].shape[0] - TILE
    masks = [mask for mask, _ in parts]

    def body(*refs):
        tokens, weights, out = refs[1 : 1 + blocks], refs[1 + blocks : -1], refs[-1]
        shards = beside(weights)
        for at in range(0, blocks, STEP):
            here = slice(at * rows, (at + STEP) * rows)
            out[here] = shard_sums(tokens[at : at + STEP], rows, refs[0][1], masks, shards)

    operands = [place, *row_blocks, *[array for _, array in parts]]
    shape = (rows * blocks, 2 * (parts[0][1].shape[0] // 3))
    return pl.pallas_call(
        body,
        out_shape=jax.ShapeDtypeStruct(shape, F32),
        in_specs=[smem()] + [vmem()] * (len(operands) - 1),
        out_specs=vmem(),
        compiler_params=params(),
        name="hidden_sums",
    )(*operands)


def expert_stage(place, own_blocks, pair_blocks, first, late, sums, picks):
    blocks = len(own_blocks)
    rows = own_blocks[0].shape[0] - TILE
    half = rows * blocks
    inner = sums.shape[1] // 2
    chunk = first[0][1].shape[1]
    parts = first + late
    width = chunk * len(parts) // 2

    def body(*refs):
        lang, seq = refs[0][0], refs[0][1]
        tokens = refs[1 : 1 + 2 * blocks]
        weights = refs[1 + 2 * blocks : -6]
        old, hidden = refs[-6], refs[-1]
        outs = refs[-5:-1]
        masks = [mask for mask, _ in parts]
        late_shards = beside(weights[len(first) :])
        shards = beside(weights)
        for at in range(0, 2 * blocks, STEP):
            group = tokens[at : at + STEP]
            if at < blocks:
                total = shard_sums(group, rows, seq, masks[len(first) :], late_shards)
                total = total + old[at * rows : (at + STEP) * rows]
            else:
                total = shard_sums(group, rows, seq, masks, shards)
            for block, ref in enumerate(group):
                fields = ref[rows:, :rows].astype(F32)
                weight = jnp.zeros((1, rows), F32)
                for pick in range(picks):
                    terms = [fields[row : row + 1] for row in range(pick, 4 * picks, picks)]
                    named = terms[0] == lang.astype(F32)
                    weight = weight + jnp.where(named, terms[1] + terms[2] + terms[3], 0.0)
                weight = jnp.broadcast_to(weight, (rows, rows)).T[:, :1]
                gate = total[block * rows : (block + 1) * rows, :inner]
                result = total[block * rows : (block + 1) * rows, inner:] * weight
                here = slice((at + block) * rows, (at + block + 1) * rows)
                hidden[here] = (gate / (1.0 + jnp.exp(-gate)) * result).astype(BF16)
        for mask, down in sorted(zip(masks, weights), key=lambda item: item[0]):
            slot = ((mask & ~1) ^ (seq & PAIR)) // 2
            cols = pl.ds(pl.multiple_of(slot * chunk, chunk), chunk)
            for at in range(0, 2 * blocks, 2 * STEP):
                here = hidden[at * rows : (at + 2 * STEP) * rows]
                result = dot(here, down[2 * inner :, :]).astype(BF16)
                for block in range(at, at + 2 * STEP):
                    target = outs[2 * (mask & 1) + block % 2]
                    piece = result[(block - at) * rows : (block - at + 1) * rows]
                    target[block // blocks, block % blocks // 2, :, cols] = piece

    arrays = [array for _, array in parts]
    operands = [place, *own_blocks, *pair_blocks, *arrays, sums]
    shape = jax.ShapeDtypeStruct((2, blocks // 2, rows, width), BF16)
    return pl.pallas_call(
        body,
        out_shape=(shape,) * 4,
        in_specs=[smem()] + [vmem()] * (len(operands) - 1),
        out_specs=(vmem(),) * 4,
        scratch_shapes=[pltpu.VMEM((2 * half, inner), BF16)],
        compiler_params=params(),
        name="expert",
    )(*operands)


def flatten(parts):
    return [array for _, arrays in parts for array in arrays]


def regroup(parts, refs):
    refs = list(refs)
    found = []
    for offset, arrays in parts:
        found.append((offset, refs[: len(arrays)]))
        refs = refs[len(arrays) :]
    return found


def attention_stage(place, table, lengths, latents, w_kv, groups):
    count, _, pages, rows, _ = latents.shape
    width = w_kv.shape[0]
    chunk = width // count
    block_rows = groups[0][1][0][1][0].shape[0]
    tokens = block_rows * count
    prompt = tokens // pages
    lat = rows * count
    keys_all = lat + prompt
    per_block = max(1, min(count, 256 * 1024 // (keys_all * rows)))
    query_rows = per_block * rows
    scale = 1.0 / math.sqrt(HD)
    rate = scale * math.log2(math.e)
    flat = [flatten(parts) for _, parts in groups]

    def body(*refs):
        own, places, used, packed, w_ref = refs[:5]
        rest = list(refs[5:])
        out, grads, mixed, prompt_grad, keys, values, key_grad, value_grad, acc = rest[-9:]
        own_place = places[0, own[1]]
        for (masks, parts), arrays in zip(groups, flat):
            for source, part_refs in regroup(parts, rest[: len(arrays)]):
                owner = places[1, (own_place + source + count) % count]
                place = pl.multiple_of(owner * block_rows, block_rows)
                for index, mask in enumerate(masks):
                    start = pl.multiple_of(((owner & ~PAIR) ^ mask) * chunk, chunk)
                    cols = slice(index * chunk, (index + 1) * chunk)
                    piece = jnp.concatenate([ref[:, cols] for ref in part_refs], axis=0)
                    mixed[pl.ds(place, block_rows), pl.ds(start, chunk)] = piece
            rest = rest[len(arrays) :]
        projected = dot(mixed[...], w_ref[...]).astype(BF16)
        for page in range(pages):
            at = slice(page * prompt, (page + 1) * prompt)
            keys[page, :lat] = packed[:, 1, page].reshape(lat, HD)
            values[page, :lat] = packed[:, 2, page].reshape(lat, HD)
            keys[page, lat:] = projected[at, :HD]
            values[page, lat:] = projected[at, HD:]

        def one_block(step, carry):
            block = pl.ds(step * per_block, per_block)
            for page in range(pages):
                query = packed[block, 0, page].reshape(query_rows, HD)
                grad = packed[block, 3, page].reshape(query_rows, HD)
                key = keys[page]
                value = values[page]
                scores = lax.dot_general(key, query, NT, preferred_element_type=F32)
                position = lax.broadcasted_iota(jnp.int32, (prompt, query_rows), 0)
                used_scores = jnp.where(position < used[page], scores[lat:], -jnp.inf)
                scores = jnp.concatenate([scores[:lat], used_scores], axis=0)
                highest = jnp.max(scores, axis=0, keepdims=True)
                raised = jnp.exp2((scores - highest) * rate)
                soft = raised * (1.0 / jnp.sum(raised, axis=0, keepdims=True))
                low = soft.astype(BF16)
                prob = lax.dot_general(value, grad, NT, preferred_element_type=F32)
                centre = jnp.sum(soft * prob, axis=0, keepdims=True)
                score_grad = (soft * (prob - centre) * scale).astype(BF16)
                attended = lax.dot_general(value, low, TN, preferred_element_type=F32).T
                query_grad = lax.dot_general(key, score_grad, TN, preferred_element_type=F32).T
                out[block, 0, page] = attended.astype(BF16).reshape(per_block, rows, HD)
                out[block, 1, page] = query_grad.astype(BF16).reshape(per_block, rows, HD)
                key_grad[page] += dot(score_grad, query)
                value_grad[page] += dot(low, grad)
            return carry

        key_grad[...] = jnp.zeros(key_grad.shape, F32)
        value_grad[...] = jnp.zeros(value_grad.shape, F32)
        lax.fori_loop(0, count // per_block, one_block, 0)
        for page in range(pages):
            out[:, 2, page] = key_grad[page, :lat].astype(BF16).reshape(count, rows, HD)
            out[:, 3, page] = value_grad[page, :lat].astype(BF16).reshape(count, rows, HD)
            at = slice(page * prompt, (page + 1) * prompt)
            prompt_grad[at, :HD] = key_grad[page, lat:].astype(BF16)
            prompt_grad[at, HD:] = value_grad[page, lat:].astype(BF16)
        total = lax.dot_general(mixed[...], prompt_grad[...], TN, preferred_element_type=F32)
        acc[pl.ds(0, width, stride=2), :] = total[:, :HD]
        acc[pl.ds(1, width, stride=2), :] = total[:, HD:]
        grads[...] = acc[...].astype(BF16)

    operands = [place, table, lengths, latents, w_kv]
    operands += [array for arrays in flat for array in arrays]
    return pl.pallas_call(
        body,
        out_shape=(
            jax.ShapeDtypeStruct(latents.shape, BF16),
            jax.ShapeDtypeStruct((2 * width, HD), BF16),
        ),
        in_specs=[smem()] * 3 + [vmem()] * (len(operands) - 3),
        out_specs=(vmem(),) * 2,
        scratch_shapes=[
            pltpu.VMEM((tokens, width), BF16),
            pltpu.VMEM((tokens, 2 * HD), BF16),
            pltpu.VMEM((pages, keys_all, HD), BF16),
            pltpu.VMEM((pages, keys_all, HD), BF16),
            pltpu.VMEM((pages, keys_all, HD), F32),
            pltpu.VMEM((pages, keys_all, HD), F32),
            pltpu.VMEM((2 * width, HD), F32),
        ],
        compiler_params=params(),
        name="attention",
    )(*operands)


def local(
    prompt_rows,
    expert_ids,
    expert_gates,
    w_gate,
    w_up,
    w_down,
    w_kv,
    prompt_lengths,
    latent_q,
    latent_k,
    latent_v,
    grad_out,
):
    count = lax.axis_size("seq")
    langs = lax.axis_size("lang")
    model_width = prompt_rows.shape[1]
    lang_index = lax.axis_index("lang")
    seq_index = lax.axis_index("seq")
    place = jnp.stack([lang_index, seq_index])
    picks = expert_ids.shape[1]

    packed = pack([latent_q, latent_k, latent_v, grad_out])
    kv_matrix = w_kv.reshape(model_width, 2 * HD)
    along, across, own_blocks, pair_blocks, first, late, sums, (packed, kv_matrix) = gather_inputs(
        w_gate[0].T,
        w_up[0].T,
        w_down[0],
        with_gates(prompt_rows, expert_ids, expert_gates),
        seq_index,
        count,
        (packed, kv_matrix),
        functools.partial(hidden_sums_stage, place),
    )
    packed = tie(packed, late[1][1])
    latents = lax.all_to_all(packed, "seq", split_axis=0, concat_axis=0, tiled=True)

    results = expert_stage(place, own_blocks, pair_blocks, first, late, sums, picks)
    groups = []
    for pair_first, members in enumerate((along, across)):
        keep, send = results[2 * pair_first : 2 * pair_first + 2]
        mixed = reduce_rows(keep, send, bool(pair_first), latents)
        groups.append((sorted(members), ring_gather(mixed, count)))

    out, part = attention_stage(
        place, ring_places(count), prompt_lengths, latents, kv_matrix, groups
    )
    returned = lax.all_to_all(out, "seq", split_axis=0, concat_axis=0, tiled=True)

    mask = langs // 2
    while mask > 1:
        part = (part.astype(F32) + xor_swap(part, "lang", mask).astype(F32)).astype(BF16)
        mask //= 2
    grad_wkv = part.astype(F32) + xor_swap(part, "lang", 1).astype(F32)
    grad_wkv = grad_wkv.reshape(model_width, 2, HD)
    attended, grad_latent = unpack(returned)
    return (attended, grad_latent, grad_wkv)


def solution(mesh):
    return jax.shard_map(
        local,
        mesh=mesh,
        in_specs=(
            P(("lang", "seq"), None),
            P(("lang", "seq"), None),
            P(("lang", "seq"), None),
            P("lang", "seq", None),
            P("lang", "seq", None),
            P("lang", None, "seq"),
            P(None, None, "seq"),
            P("lang"),
            P("lang", "seq", None),
            P("lang", "seq", None),
            P("lang", "seq", None),
            P("lang", "seq", None),
        ),
        out_specs=(P("lang", "seq", None), P(None, "lang", "seq", None), P(None, None, "seq")),
        check_vma=False,
    )
```

```python
import functools
import math

import jax
import jax.numpy as jnp
from jax import lax
from jax.experimental import pallas as pl
from jax.experimental.pallas import tpu as pltpu
from jax.sharding import PartitionSpec as P

HD = 128
PAIR = 2
TILE = 16
STEP = 4
NT = (((1,), (1,)), ((), ()))
TN = (((0,), (0,)), ((), ()))
F32 = jnp.float32
BF16 = jnp.bfloat16


def params():
    return pltpu.CompilerParams(vmem_limit_bytes=60 * 2**20)


def vmem():
    return pl.BlockSpec(memory_space=pltpu.VMEM)


def smem():
    return pl.BlockSpec(memory_space=pltpu.SMEM)


def dot(a, b):
    return jnp.dot(a, b, preferred_element_type=F32)


def ring_order(count):
    return list(range(0, count, 2)) + list(range(count - 1, 0, -2))


def ring_pairs(count, step):
    order = ring_order(count)
    return [(order[i], order[(i + step) % count]) for i in range(count)]


def ring_places(count):
    order = ring_order(count)
    return jnp.array([[order.index(i) for i in range(count)], order], jnp.int32)


def ring_gather(block, count):
    ahead = ring_pairs(count, 1)
    back = ring_pairs(count, -1)
    half_rows = block.shape[0] // 2
    parts = [(0, [block])]
    up, down = block, block
    for distance in range(1, count // 2):
        up = lax.ppermute(up, "seq", ahead)
        down = lax.ppermute(down, "seq", back)
        parts.append((-distance, [up]))
        parts.append((distance, [down]))
    last_up = lax.ppermute(up[:half_rows], "seq", ahead)
    last_down = lax.ppermute(down[half_rows:], "seq", back)
    parts.append((count // 2, [last_up, last_down]))
    return parts


def whole(refs):
    if len(refs) == 1:
        return refs[0][...]
    return jnp.concatenate([ref[...] for ref in refs], axis=0)


def xor_swap(array, axis, mask):
    count = lax.axis_size(axis)
    return lax.ppermute(array, axis, [(i, i ^ mask) for i in range(count)])


def gather_lang(rows, far):
    langs = lax.axis_size("lang")
    mask = langs // 2
    blocks = {0: rows, mask: far}
    while mask > 1:
        mask //= 2
        for lang, block in list(blocks.items()):
            blocks[lang | mask] = xor_swap(block, "lang", mask)
    return [blocks[lang] for lang in range(langs)]


def reduce_rows(keep, send, pair_first, after):
    langs = lax.axis_size("lang")

    def over_pair(parts):
        kept, sent = parts
        arrived = xor_swap(tie(sent.astype(BF16), after), "seq", PAIR)
        return kept + arrived.astype(F32)

    arrived = xor_swap(send, "lang", 1)
    halves = [keep[side].astype(F32) + arrived[side].astype(F32) for side in range(2)]
    if pair_first:
        halves = [over_pair(halves)]
    mask = 2
    while mask < langs:
        sent = jnp.stack([half[1::2] for half in halves]).astype(BF16)
        arrived = xor_swap(sent, "lang", mask).astype(F32)
        halves = [half[0::2] + arrived[side] for side, half in enumerate(halves)]
        mask *= 2
    total = halves[0] if pair_first else over_pair(halves)
    return total[0].astype(BF16)


def split_halves(block, seq_index):
    rows = block.shape[0] // 2
    side = (seq_index // PAIR) % 2
    mine = lax.dynamic_slice_in_dim(block, side * rows, rows, 0)
    other = lax.dynamic_slice_in_dim(block, (1 - side) * rows, rows, 0)
    return mine, other


def tie(array, *others):
    return lax.optimization_barrier((array, *others))[0]


def gather_inputs(gate, up, down, rows, seq_index, count, aside, own_sums):
    top = lax.axis_size("lang") // 2
    mine, other = zip(*[split_halves(block, seq_index) for block in (gate, up, down)])
    mine = jnp.concatenate(mine, axis=0)
    other = jnp.concatenate(other, axis=0)
    along, across = {0: mine}, {}
    along[2 * PAIR] = xor_swap(mine, "seq", 2 * PAIR)
    along[PAIR] = xor_swap(other, "seq", PAIR)
    across[1] = xor_swap(mine, "seq", 1)
    ready = [2 * PAIR, PAIR]
    pair_rows = far = rows
    for mask in range(3 * PAIR, count, PAIR):
        held = other if mask & PAIR else mine
        arrived = [along[done] for done in ready]
        held, pair_rows, far, across[1], aside, arrived = lax.optimization_barrier(
            (held, pair_rows, far, across[1], aside, arrived)
        )
        along[mask] = xor_swap(held, "seq", mask)
        for done, array in zip(ready, arrived):
            along[done] = array
            across[done | 1] = xor_swap(array, "seq", 1)
        if mask == 3 * PAIR:
            pair_rows = xor_swap(pair_rows, "seq", PAIR)
            far = xor_swap(far, "lang", top)
        ready = [mask]
    last = ready[0]
    early = [across[mask | 1] for mask in along if mask not in (0, last)]
    pair_rows, far, along[last], early = lax.optimization_barrier(
        (pair_rows, far, along[last], early)
    )
    for mask, array in zip([mask for mask in along if mask not in (0, last)], early):
        across[mask | 1] = array
    own_blocks = gather_lang(rows, far)
    first = sorted((along | across).items())
    first = [item for item in first if item[0] != last]
    sums = own_sums(own_blocks, first)
    across[last | 1], pair_far, sums = lax.optimization_barrier(
        (xor_swap(along[last], "seq", 1), xor_swap(pair_rows, "lang", top), sums)
    )
    pair_blocks = gather_lang(pair_rows, pair_far)
    late = [(mask, shard) for mask, shard in ((last, along[last]), (last | 1, across[last | 1]))]
    return along, across, own_blocks, pair_blocks, first, late, sums, aside


def pack_body(*refs):
    out = refs[-1]
    for which, ref in enumerate(refs[:-1]):
        for head in range(out.shape[0]):
            out[head, which] = ref[:, :, head * HD : (head + 1) * HD]


def pack(arrays):
    pages, rows, width = arrays[0].shape
    shape = (width // HD, len(arrays), pages, rows, HD)
    return pl.pallas_call(
        pack_body,
        out_shape=jax.ShapeDtypeStruct(shape, BF16),
        in_specs=[vmem()] * len(arrays),
        out_specs=vmem(),
        compiler_params=params(),
        name="pack",
    )(*arrays)


def unpack(packed):
    heads = range(packed.shape[0])
    attended = jnp.concatenate([packed[head, 0] for head in heads], axis=-1)
    return attended, jnp.concatenate([packed[head, 1:] for head in heads], axis=-1)


def with_gates(rows, expert_ids, expert_gates):
    picks = expert_ids.shape[1]
    fields = [expert_ids.T.astype(F32)]
    rest = expert_gates.T
    for _ in range(3):
        term = lax.reduce_precision(rest, 8, 7)
        fields.append(term)
        rest = rest - term
    tile = jnp.concatenate(fields, axis=0).astype(BF16)
    tile = jnp.pad(tile, ((0, TILE - 4 * picks), (0, rows.shape[1] - rows.shape[0])))
    return jnp.concatenate([rows, tile], axis=0)


def shard_sums(tokens, rows, seq, masks, shards):
    chunk = shards.shape[1] // len(masks)
    starts = [pl.multiple_of((seq ^ mask) * chunk, chunk) for mask in masks]
    inputs = [
        jnp.concatenate([ref[:rows, pl.ds(start, chunk)] for start in starts], axis=1)
        for ref in tokens
    ]
    inputs = jnp.concatenate(inputs, axis=0)
    return lax.dot_general(inputs, shards, NT, preferred_element_type=F32)


def beside(weights):
    both = 2 * (weights[0].shape[0] // 3)
    return jnp.concatenate([weight[:both, :] for weight in weights], axis=1)


def hidden_sums_stage(place, row_blocks, parts):
    blocks = len(row_blocks)
    rows = row_blocks[0].shape[0] - TILE
    masks = [mask for mask, _ in parts]

    def body(*refs):
        tokens, weights, out = refs[1 : 1 + blocks], refs[1 + blocks : -1], refs[-1]
        shards = beside(weights)
        for at in range(0, blocks, STEP):
            here = slice(at * rows, (at + STEP) * rows)
            out[here] = shard_sums(tokens[at : at + STEP], rows, refs[0][1], masks, shards)

    operands = [place, *row_blocks, *[array for _, array in parts]]
    shape = (rows * blocks, 2 * (parts[0][1].shape[0] // 3))
    return pl.pallas_call(
        body,
        out_shape=jax.ShapeDtypeStruct(shape, F32),
        in_specs=[smem()] + [vmem()] * (len(operands) - 1),
        out_specs=vmem(),
        compiler_params=params(),
        name="hidden_sums",
    )(*operands)


def expert_stage(place, own_blocks, pair_blocks, first, late, sums, picks):
    blocks = len(own_blocks)
    rows = own_blocks[0].shape[0] - TILE
    half = rows * blocks
    inner = sums.shape[1] // 2
    chunk = first[0][1].shape[1]
    parts = first + late
    width = chunk * len(parts) // 2

    def body(*refs):
        lang, seq = refs[0][0], refs[0][1]
        tokens = refs[1 : 1 + 2 * blocks]
        weights = refs[1 + 2 * blocks : -6]
        old, hidden = refs[-6], refs[-1]
        outs = refs[-5:-1]
        masks = [mask for mask, _ in parts]
        late_shards = beside(weights[len(first) :])
        shards = beside(weights)
        for at in range(0, 2 * blocks, STEP):
            group = tokens[at : at + STEP]
            if at < blocks:
                total = shard_sums(group, rows, seq, masks[len(first) :], late_shards)
                total = total + old[at * rows : (at + STEP) * rows]
            else:
                total = shard_sums(group, rows, seq, masks, shards)
            for block, ref in enumerate(group):
                fields = ref[rows:, :rows].astype(F32)
                weight = jnp.zeros((1, rows), F32)
                for pick in range(picks):
                    terms = [fields[row : row + 1] for row in range(pick, 4 * picks, picks)]
                    named = terms[0] == lang.astype(F32)
                    weight = weight + jnp.where(named, terms[1] + terms[2] + terms[3], 0.0)
                weight = jnp.broadcast_to(weight, (rows, rows)).T[:, :1]
                gate = total[block * rows : (block + 1) * rows, :inner]
                result = total[block * rows : (block + 1) * rows, inner:] * weight
                here = slice((at + block) * rows, (at + block + 1) * rows)
                hidden[here] = (gate / (1.0 + jnp.exp(-gate)) * result).astype(BF16)
        for mask, down in sorted(zip(masks, weights), key=lambda item: item[0]):
            slot = ((mask & ~1) ^ (seq & PAIR)) // 2
            cols = pl.ds(pl.multiple_of(slot * chunk, chunk), chunk)
            for at in range(0, 2 * blocks, 2 * STEP):
                here = hidden[at * rows : (at + 2 * STEP) * rows]
                result = dot(here, down[2 * inner :, :]).astype(BF16)
                for block in range(at, at + 2 * STEP):
                    target = outs[2 * (mask & 1) + block % 2]
                    piece = result[(block - at) * rows : (block - at + 1) * rows]
                    target[block // blocks, block % blocks // 2, :, cols] = piece

    arrays = [array for _, array in parts]
    operands = [place, *own_blocks, *pair_blocks, *arrays, sums]
    shape = jax.ShapeDtypeStruct((2, blocks // 2, rows, width), BF16)
    return pl.pallas_call(
        body,
        out_shape=(shape,) * 4,
        in_specs=[smem()] + [vmem()] * (len(operands) - 1),
        out_specs=(vmem(),) * 4,
        scratch_shapes=[pltpu.VMEM((2 * half, inner), BF16)],
        compiler_params=params(),
        name="expert",
    )(*operands)


def flatten(parts):
    return [array for _, arrays in parts for array in arrays]


def regroup(parts, refs):
    refs = list(refs)
    found = []
    for offset, arrays in parts:
        found.append((offset, refs[: len(arrays)]))
        refs = refs[len(arrays) :]
    return found


def attention_stage(place, table, lengths, latents, w_kv, groups):
    count, _, pages, rows, _ = latents.shape
    width = w_kv.shape[0]
    chunk = width // count
    block_rows = groups[0][1][0][1][0].shape[0]
    tokens = block_rows * count
    prompt = tokens // pages
    lat = rows * count
    keys_all = lat + prompt
    per_block = max(1, min(count, 256 * 1024 // (keys_all * rows)))
    query_rows = per_block * rows
    scale = 1.0 / math.sqrt(HD)
    rate = scale * math.log2(math.e)
    flat = [flatten(parts) for _, parts in groups]

    def body(*refs):
        own, places, used, packed, w_ref = refs[:5]
        rest = list(refs[5:])
        out, grads, mixed, prompt_grad, keys, values, key_grad, value_grad, acc = rest[-9:]
        own_place = places[0, own[1]]
        for (masks, parts), arrays in zip(groups, flat):
            for source, part_refs in regroup(parts, rest[: len(arrays)]):
                owner = places[1, (own_place + source + count) % count]
                place = pl.multiple_of(owner * block_rows, block_rows)
                for index, mask in enumerate(masks):
                    start = pl.multiple_of(((owner & ~PAIR) ^ mask) * chunk, chunk)
                    cols = slice(index * chunk, (index + 1) * chunk)
                    piece = jnp.concatenate([ref[:, cols] for ref in part_refs], axis=0)
                    mixed[pl.ds(place, block_rows), pl.ds(start, chunk)] = piece
            rest = rest[len(arrays) :]
        projected = dot(mixed[...], w_ref[...]).astype(BF16)
        for page in range(pages):
            at = slice(page * prompt, (page + 1) * prompt)
            keys[page, :lat] = packed[:, 1, page].reshape(lat, HD)
            values[page, :lat] = packed[:, 2, page].reshape(lat, HD)
            keys[page, lat:] = projected[at, :HD]
            values[page, lat:] = projected[at, HD:]

        def one_block(step, carry):
            block = pl.ds(step * per_block, per_block)
            for page in range(pages):
                query = packed[block, 0, page].reshape(query_rows, HD)
                grad = packed[block, 3, page].reshape(query_rows, HD)
                key = keys[page]
                value = values[page]
                scores = lax.dot_general(key, query, NT, preferred_element_type=F32)
                position = lax.broadcasted_iota(jnp.int32, (prompt, query_rows), 0)
                used_scores = jnp.where(position < used[page], scores[lat:], -jnp.inf)
                scores = jnp.concatenate([scores[:lat], used_scores], axis=0)
                highest = jnp.max(scores, axis=0, keepdims=True)
                raised = jnp.exp2((scores - highest) * rate)
                soft = raised * (1.0 / jnp.sum(raised, axis=0, keepdims=True))
                low = soft.astype(BF16)
                prob = lax.dot_general(value, grad, NT, preferred_element_type=F32)
                centre = jnp.sum(soft * prob, axis=0, keepdims=True)
                score_grad = (soft * (prob - centre) * scale).astype(BF16)
                attended = lax.dot_general(value, low, TN, preferred_element_type=F32).T
                query_grad = lax.dot_general(key, score_grad, TN, preferred_element_type=F32).T
                out[block, 0, page] = attended.astype(BF16).reshape(per_block, rows, HD)
                out[block, 1, page] = query_grad.astype(BF16).reshape(per_block, rows, HD)
                key_grad[page] += dot(score_grad, query)
                value_grad[page] += dot(low, grad)
            return carry

        key_grad[...] = jnp.zeros(key_grad.shape, F32)
        value_grad[...] = jnp.zeros(value_grad.shape, F32)
        lax.fori_loop(0, count // per_block, one_block, 0)
        for page in range(pages):
            out[:, 2, page] = key_grad[page, :lat].astype(BF16).reshape(count, rows, HD)
            out[:, 3, page] = value_grad[page, :lat].astype(BF16).reshape(count, rows, HD)
            at = slice(page * prompt, (page + 1) * prompt)
            prompt_grad[at, :HD] = key_grad[page, lat:].astype(BF16)
            prompt_grad[at, HD:] = value_grad[page, lat:].astype(BF16)
        total = lax.dot_general(mixed[...], prompt_grad[...], TN, preferred_element_type=F32)
        acc[pl.ds(0, width, stride=2), :] = total[:, :HD]
        acc[pl.ds(1, width, stride=2), :] = total[:, HD:]
        grads[...] = acc[...].astype(BF16)

    operands = [place, table, lengths, latents, w_kv]
    operands += [array for arrays in flat for array in arrays]
    return pl.pallas_call(
        body,
        out_shape=(
            jax.ShapeDtypeStruct(latents.shape, BF16),
            jax.ShapeDtypeStruct((2 * width, HD), BF16),
        ),
        in_specs=[smem()] * 3 + [vmem()] * (len(operands) - 3),
        out_specs=(vmem(),) * 2,
        scratch_shapes=[
            pltpu.VMEM((tokens, width), BF16),
            pltpu.VMEM((tokens, 2 * HD), BF16),
            pltpu.VMEM((pages, keys_all, HD), BF16),
            pltpu.VMEM((pages, keys_all, HD), BF16),
            pltpu.VMEM((pages, keys_all, HD), F32),
            pltpu.VMEM((pages, keys_all, HD), F32),
            pltpu.VMEM((2 * width, HD), F32),
        ],
        compiler_params=params(),
        name="attention",
    )(*operands)


def local(
    prompt_rows,
    expert_ids,
    expert_gates,
    w_gate,
    w_up,
    w_down,
    w_kv,
    prompt_lengths,
    latent_q,
    latent_k,
    latent_v,
    grad_out,
):
    count = lax.axis_size("seq")
    langs = lax.axis_size("lang")
    model_width = prompt_rows.shape[1]
    lang_index = lax.axis_index("lang")
    seq_index = lax.axis_index("seq")
    place = jnp.stack([lang_index, seq_index])
    picks = expert_ids.shape[1]

    packed = pack([latent_q, latent_k, latent_v, grad_out])
    kv_matrix = w_kv.reshape(model_width, 2 * HD)
    along, across, own_blocks, pair_blocks, first, late, sums, (packed, kv_matrix) = gather_inputs(
        w_gate[0].T,
        w_up[0].T,
        w_down[0],
        with_gates(prompt_rows, expert_ids, expert_gates),
        seq_index,
        count,
        (packed, kv_matrix),
        functools.partial(hidden_sums_stage, place),
    )
    packed = tie(packed, late[1][1])
    latents = lax.all_to_all(packed, "seq", split_axis=0, concat_axis=0, tiled=True)

    results = expert_stage(place, own_blocks, pair_blocks, first, late, sums, picks)
    groups = []
    for pair_first, members in enumerate((along, across)):
        keep, send = results[2 * pair_first : 2 * pair_first + 2]
        mixed = reduce_rows(keep, send, bool(pair_first), latents)
        groups.append((sorted(members), ring_gather(mixed, count)))

    out, part = attention_stage(
        place, ring_places(count), prompt_lengths, latents, kv_matrix, groups
    )
    returned = lax.all_to_all(out, "seq", split_axis=0, concat_axis=0, tiled=True)

    mask = langs // 2
    while mask > 1:
        part = (part.astype(F32) + xor_swap(part, "lang", mask).astype(F32)).astype(BF16)
        mask //= 2
    grad_wkv = part.astype(F32) + xor_swap(part, "lang", 1).astype(F32)
    grad_wkv = grad_wkv.reshape(model_width, 2, HD)
    attended, grad_latent = unpack(returned)
    return (attended, grad_latent, grad_wkv)


def solution(mesh):
    return jax.shard_map(
        local,
        mesh=mesh,
        in_specs=(
            P(("lang", "seq"), None),
            P(("lang", "seq"), None),
            P(("lang", "seq"), None),
            P("lang", "seq", None),
            P("lang", "seq", None),
            P("lang", None, "seq"),
            P(None, None, "seq"),
            P("lang"),
            P("lang", "seq", None),
            P("lang", "seq", None),
            P("lang", "seq", None),
            P("lang", "seq", None),
        ),
        out_specs=(P("lang", "seq", None), P(None, "lang", "seq", None), P(None, None, "seq")),
        check_vma=False,
    )
```
